256 devices in a mesh: row: 8 (over z_lo, core), col: 32 (over z_hi, y, x).
Axes of the slice: x: 4, y: 4, z: 8 (z_hi: 2, z_lo: 4; z = z_hi * 4 + z_lo), core: 2. Of those that a mesh axis runs over, the one named last changes fastest.
Arguments:
- observations: float32 [8192, 16, 4096], P('row', None, 'col'), may hold values from -6 to 6
- prior_rows: float32 [256, 16, 4096], P(None, 'row', 'col'), may hold values from -8 to 96, as said below
Outputs:
- updated_rows: float32 [256, 16, 4096], P(None, 'row', 'col')
The draws below stay inside these ranges and needn't reach their ends.
Inputs may be any that keep to these rules, and one draw needn't show every extreme that they name: `prior_rows`: entry (i, c, q) is zero where its global column is below i, lies in [32, 96] where the global column equals i, and elsewhere lies in [-8, 8].
All inputs are finite; a program needn't handle non-finite values.
Results may differ from the reference program's by a relative error of at most 0.0001.
Values sent between devices are 32-bit elements; how exact they have to be, the bound alone decides.
No kernel may reach another device: no remote copies, remote signals or barrier semaphores. Data moves between devices by JAX's collectives and lax.ppermute only.
A program may use at most 128 MiB of HBM per device.

```python
import jax
import jax.numpy as jnp
from jax import lax

N = 65536
PANEL_COLUMNS = 128
PANELS = 2
OBS = 8192
RROWS = 256
CYC = 16
N_COL = 32


def draw_prior_rows(key, part):
    key = jax.random.fold_in(key, 7)
    upper_key, diag_key = jax.random.split(key)
    row_ids = lax.broadcasted_iota(jnp.int32, (RROWS, N), 0)
    col_ids = lax.broadcasted_iota(jnp.int32, (RROWS, N), 1)
    upper_vals = jnp.clip(2.0 * jax.random.normal(upper_key, (RROWS, N), jnp.float32), -8.0, 8.0)
    diag_vals = jax.random.uniform(diag_key, (RROWS, N), jnp.float32, 32.0, 96.0)
    values = jnp.where(col_ids > row_ids, upper_vals, jnp.where(col_ids == row_ids, diag_vals, jnp.float32(0.0)))
    return values.reshape(RROWS, CYC, N // CYC)


def block_levels(own_key, dims, cuts, smallest, top_value):
    def one(dim, shards_of):
        heights = jax.random.uniform(jax.random.fold_in(jax.random.fold_in(own_key, 6), dim), (shards_of,), jnp.float32, smallest / len(cuts), top_value / len(cuts))
        return jnp.repeat(jnp.exp(heights), dims[dim] // shards_of).reshape((-1,) + (1,) * (len(dims) - dim - 1))

    loudness = one(*cuts[0])
    for cut in cuts[1:]:
        loudness = loudness * one(*cut)
    return loudness


def centred(own_key, extent, deviation, reach, shards=(), kind=jnp.bfloat16):
    array = jax.random.normal(own_key, extent, jnp.float32) * deviation
    if len(shards) > 0:
        array = block_levels(own_key, extent, shards, -0.22, 0.18) * array
    return jnp.clip(array, min=-reach, max=reach).astype(kind)


def setup_inputs(seed: int = 0) -> dict:
    key_list = jax.random.split(jax.random.key(seed), 3)
    observations = centred(key_list[0], (OBS, CYC, N_COL * PANEL_COLUMNS), 1.0, 6.0, ((0, 8), (2, 32)), jnp.float32)
    prior_rows = draw_prior_rows(jax.random.fold_in(key_list[2], 71), 0)
    return {"observations": observations, "prior_rows": prior_rows}


highest_precision = lax.Precision.HIGHEST

def reference(observations, prior_rows):
    measurement_rows = observations
    prior_factor_rows = prior_rows
    width = N_COL * PANEL_COLUMNS
    results = []
    block_ids = lax.broadcasted_iota(jnp.int32, (1, CYC, width), 1) * N_COL + lax.broadcasted_iota(jnp.int32, (1, CYC, width), 2) // PANEL_COLUMNS
    for panel_number_index in range(PANELS):
        rotation_index = panel_number_index * PANEL_COLUMNS // width
        column_offset = panel_number_index * PANEL_COLUMNS % width
        panel_measurement = measurement_rows[:, rotation_index, column_offset:column_offset + PANEL_COLUMNS]
        panel_prior_rows = prior_factor_rows[:, rotation_index, column_offset:column_offset + PANEL_COLUMNS]
        total_gram_matrix = jnp.dot(panel_measurement.T, panel_measurement, precision=highest_precision) + jnp.dot(panel_prior_rows.T, panel_prior_rows, precision=highest_precision)
        lower_cholesky = jnp.linalg.cholesky(total_gram_matrix)
        measurement_basis = jax.scipy.linalg.solve_triangular(lower_cholesky, panel_measurement.T, lower=True).T
        basis_row_block = jax.scipy.linalg.solve_triangular(lower_cholesky, panel_prior_rows.T, lower=True).T
        panel_coefficients = jnp.einsum('sd,slb->dlb', measurement_basis, measurement_rows, precision=highest_precision) + jnp.einsum('sd,slb->dlb', basis_row_block, prior_factor_rows, precision=highest_precision)
        results.append(jnp.where(block_ids >= panel_number_index, panel_coefficients, jnp.float32(0.0)))
        if panel_number_index + 1 < PANELS:
            measurement_rows = measurement_rows - jnp.einsum('hv,vjp->hjp', measurement_basis, panel_coefficients, precision=highest_precision)
            prior_factor_rows = prior_factor_rows - jnp.einsum('hv,vjp->hjp', basis_row_block, panel_coefficients, precision=highest_precision)
    return jnp.concatenate(results, axis=0)
```

```python
import jax
import jax.numpy as jnp
from jax import lax
from jax.experimental import pallas as pl
from jax.experimental.pallas import tpu as pltpu
from jax.sharding import PartitionSpec as P

F32 = jnp.float32
BF16 = jnp.bfloat16
HIGHEST = lax.Precision.HIGHEST
ANY_CONTRACT = (((0,), (0,)), ((), ()))


def dot_tt(a, b):
    return lax.dot_general(a, b, ANY_CONTRACT, precision=HIGHEST, preferred_element_type=F32)


def dot(a, b):
    return jnp.dot(a, b, precision=HIGHEST, preferred_element_type=F32)


def split2(x):
    hi = x.astype(BF16)
    return hi, (x - hi.astype(F32)).astype(BF16)


def split3(x):
    one = x.astype(BF16).astype(F32)
    rest = x - one
    two = rest.astype(BF16).astype(F32)
    return one, two, rest - two


def eliminate(a_ref, u_ref, n):
    sub = lax.broadcasted_iota(jnp.int32, (8, n), 0)
    for k in range(n // 8):
        lo = 8 * k
        left = a_ref[lo : lo + 8, :n]
        right = a_ref[lo : lo + 8, n:]
        rl = [jnp.broadcast_to(left[p : p + 1, :], (8, n)) for p in range(8)]
        rr = [jnp.broadcast_to(right[p : p + 1, :], (8, n)) for p in range(8)]
        d = [
            [
                jnp.broadcast_to(left[p : p + 1, lo + q : lo + q + 1], (8, n)) if q >= p else None
                for q in range(8)
            ]
            for p in range(8)
        ]
        tl = tr = None
        for p in range(8):
            inv = 1.0 / d[p][p]
            rs = lax.rsqrt(d[p][p])
            rs = rs * (1.5 - 0.5 * d[p][p] * rs * rs)
            for q in range(p + 1, 8):
                factor = d[p][q] * inv
                for s in range(q, 8):
                    d[q][s] = d[q][s] - factor * d[p][s]
                rl[q] = rl[q] - factor * rl[p]
                rr[q] = rr[q] - factor * rr[p]
            a = rl[p] * rs
            b = rr[p] * rs
            tl = a if p == 0 else jnp.where(sub == p, a, tl)
            tr = b if p == 0 else jnp.where(sub == p, b, tr)
        u_ref[lo : lo + 8, :n] = tl
        u_ref[lo : lo + 8, n:] = tr
        if k + 1 < n // 8:
            t1, t2, t3 = split3(jnp.concatenate([tl, tr], axis=1))
            lhs = jnp.concatenate([t1[:, :n], t1[:, :n], t2[:, :n], t1[:, :n], t2[:, :n], t3[:, :n]], axis=0)
            rhs = jnp.concatenate([t1, t2, t1, t3, t2, t1], axis=0)
            update = lax.dot_general(
                lhs.astype(BF16), rhs.astype(BF16), ANY_CONTRACT, preferred_element_type=F32
            )
            a_ref[lo + 8 :, :] = a_ref[lo + 8 :, :] - update[lo + 8 :, :]


def factor_kernel(ids_ref, kept_ref, other_ref, w_ref, a_ref, u_ref):
    h = kept_ref.shape[0]
    first = ids_ref[1] == 0
    eye = (
        lax.broadcasted_iota(jnp.int32, (h, h), 0) == lax.broadcasted_iota(jnp.int32, (h, h), 1)
    ).astype(F32)
    top = jnp.where(first, kept_ref[...], other_ref[...])
    bottom = jnp.where(first, other_ref[:, h:], kept_ref[:, h:])
    a_ref[:, :h] = top[:, :h]
    a_ref[:, h:] = eye
    eliminate(a_ref, u_ref, h)
    w00 = u_ref[:, h:]
    w_ref[:h, :h] = w00
    w_ref[:h, h:] = jnp.zeros((h, h), F32)
    u01 = dot(w00, top[:, h:])
    a_ref[:, :h] = bottom - dot_tt(u01, u01)
    a_ref[:, h:] = eye
    x = dot_tt(u01, w00)
    eliminate(a_ref, u_ref, h)
    w11 = u_ref[:, h:]
    w_ref[h:, h:] = w11
    w_ref[h:, :h] = -dot(w11, x)


def split_kernel(obs_ref, hi_ref, lo_ref):
    for c in range(obs_ref.shape[1]):
        hi, lo = split2(obs_ref[:, c, :])
        hi_ref[c] = hi
        lo_ref[c] = lo


def panel_kernel(ids_ref, z_ref, hi_ref, lo_ref, keep_ref, send_ref, prior_ref, p_ref):
    pieces, panels, rows, width = z_ref.shape
    obs_rows = p_ref.shape[0] // pieces
    pri_rows = rows - obs_rows
    holder = ids_ref[0] == 0
    for i in range(pieces):
        for p in range(panels):
            p_ref[obs_rows * i : obs_rows * (i + 1), width * p : width * (p + 1)] = z_ref[i, p, :obs_rows, :]
            prior_ref[pri_rows * i : pri_rows * (i + 1), width * p : width * (p + 1)] = z_ref[i, p, obs_rows:, :]
    prior = jnp.where(holder, prior_ref[...], 0.0)
    panel = p_ref[...]
    turned = panel.T
    hi, lo = split2(turned)
    hi_ref[...] = hi
    lo_ref[...] = lo
    gram = dot(turned, panel) + dot_tt(prior, prior)
    half = gram.shape[0] // 2
    low = ids_ref[1] == 0
    keep_ref[...] = jnp.where(low, gram[:half], gram[half:])
    send_ref[...] = jnp.where(low, gram[half:], gram[:half])


def product_kernel(ids_ref, other, phi_ref, plo_ref, ahi_ref, alo_ref, out_ref):
    places, own, _, _ = out_ref.shape
    core = ids_ref[1]
    side = 1 - core if other else core
    phi = phi_ref[...]
    plo = plo_ref[...]

    def one(t, carry):
        z = t // own
        e = t % own
        c = (2 * z + side) * own + e
        hi = ahi_ref[c]
        lo = alo_ref[c]
        out_ref[z, e] = (
            jnp.dot(phi, hi, preferred_element_type=F32)
            + jnp.dot(phi, lo, preferred_element_type=F32)
            + jnp.dot(plo, hi, preferred_element_type=F32)
        )
        return carry

    lax.fori_loop(0, places * own, one, 0)


def combine_kernel(ids_ref, kept_ref, got_ref, *out_refs):
    z = ids_ref[0] // 2
    for k, out_ref in enumerate(out_refs):
        at = jnp.bitwise_xor(z, k)
        out_ref[...] = kept_ref[at] + got_ref[at]


def prior_kernel(panel_ref, own_ref, out_ref):
    for c in range(own_ref.shape[1]):
        out_ref[c] = dot_tt(panel_ref[...], own_ref[:, c, :])


def finish_kernel(n_col, ids_ref, w_ref, q_ref, a_ref, b_ref, c_ref, d_ref, out_ref):
    own, rows, width = q_ref.shape
    row_pos = ids_ref[0]
    col_pos = ids_ref[2]
    w = w_ref[...]
    for c in range(own):
        total = ((a_ref[c] + b_ref[c]) + (c_ref[c] + d_ref[c])) + q_ref[c]
        coeffs = dot(w, total)
        panel = lax.broadcasted_iota(jnp.int32, (rows, width), 0) // width
        block = (row_pos * own + c) * n_col + col_pos
        out_ref[:, c, :] = jnp.where(block >= panel, coeffs, 0.0)


def smem():
    return pl.BlockSpec(memory_space=pltpu.SMEM)


def vmem():
    return pl.BlockSpec(memory_space=pltpu.VMEM)


def call(kernel, name, out_shape, ids, *args, scratch=(), limit=48 << 20):
    return pl.pallas_call(
        kernel,
        out_shape=out_shape,
        in_specs=[smem()] + [vmem()] * len(args),
        out_specs=jax.tree.map(lambda _: vmem(), out_shape),
        scratch_shapes=list(scratch),
        compiler_params=pltpu.CompilerParams(vmem_limit_bytes=limit),
        name=name,
    )(ids, *args)


def struct(shape, dtype=F32):
    return jax.ShapeDtypeStruct(shape, dtype)


def local(observations, prior_rows):
    obs, cycles, width = observations.shape
    total_rows, own, _ = prior_rows.shape
    panels = total_rows // width
    n_row = lax.axis_size("row")
    n_col = lax.axis_size("col")
    plane = n_col // 2
    places = n_row // 2
    row_pos = lax.axis_index("row")
    col_pos = lax.axis_index("col")
    core = row_pos % 2
    ids = jnp.stack([row_pos, core, col_pos]).astype(jnp.int32)

    pieces = jnp.concatenate(
        [
            observations[:, 0, :].reshape(plane, obs // plane, width),
            prior_rows[:, 0, :].reshape(plane, total_rows // plane, width),
        ],
        axis=1,
    )
    planes = [[h * plane + i for i in range(plane)] for h in range(2)]
    got = lax.all_to_all(pieces, "col", 0, 0, tiled=True, axis_index_groups=planes)[:panels]
    far = lax.ppermute(got, "col", [(i, i + plane) for i in range(plane)])

    steps = 8
    ahi, alo = pl.pallas_call(
        split_kernel,
        grid=(steps,),
        in_specs=[pl.BlockSpec((obs // steps, cycles, width), lambda i: (i, 0, 0))],
        out_specs=[pl.BlockSpec((cycles, obs // steps, width), lambda i: (0, i, 0))] * 2,
        out_shape=[struct((cycles, obs, width), BF16)] * 2,
        name="split",
    )(observations)

    mine = jnp.where(col_pos >= plane, far, got)
    rows = mine.shape[1]
    spread = jnp.broadcast_to(mine[None], (plane, panels, rows, width))
    gathered = lax.all_to_all(spread, "col", 0, 0, tiled=True, axis_index_groups=planes)

    wide = panels * width
    phi, plo, gram_keep, gram_send, prior_panel = call(
        panel_kernel,
        "panel",
        [
            struct((wide, obs), BF16),
            struct((wide, obs), BF16),
            struct((wide // 2, wide)),
            struct((wide // 2, wide)),
            struct((total_rows, wide)),
        ],
        ids,
        gathered,
        scratch=[pltpu.VMEM((obs, wide), F32)],
    )

    def swap(x, k):
        return lax.ppermute(x, "row", [(r, r ^ k) for r in range(n_row)])

    gram = gram_keep + swap(gram_send, 1)

    def product(other):
        return call(
            lambda *refs: product_kernel(refs[0], other, *refs[1:]),
            "product_send" if other else "product_keep",
            struct((places, own, wide, width)),
            ids,
            phi,
            plo,
            ahi,
            alo,
        )

    sums_send = product(True)
    sums_got = swap(sums_send, 1)
    gram = gram + swap(gram, 2)
    gram = gram + swap(gram, 4)
    gram_other = swap(gram, 1)
    sums_keep = product(False)

    to = call(
        combine_kernel,
        "combine",
        [struct((own, wide, width))] * places,
        ids,
        sums_keep,
        sums_got,
    )
    came = [swap(to[k], 2 * k) for k in range(1, places)]

    w = call(
        factor_kernel,
        "factor",
        struct((wide, wide)),
        ids,
        gram,
        gram_other,
        scratch=[pltpu.VMEM((wide // 2, wide), F32)] * 2,
    )

    def hand(x, pairs):
        moved = lax.ppermute(x, "row", pairs)
        takes = jnp.zeros((), jnp.bool_)
        for _, dst in pairs:
            takes = takes | (row_pos == dst)
        return jnp.where(takes, moved, x)

    full = hand(prior_panel, [(0, 1)])
    part = lax.dynamic_slice_in_dim(full, core * (total_rows // 2), total_rows // 2, 0)
    part = hand(part, [(0, 4), (1, 5)])
    part = hand(part, [(0, 2), (1, 3), (4, 6), (5, 7)])
    rest = swap(part, 1)
    prior_full = jnp.where(
        core == 0, jnp.concatenate([part, rest], axis=0), jnp.concatenate([rest, part], axis=0)
    )
    q = pl.pallas_call(
        prior_kernel,
        out_shape=struct((own, wide, width)),
        name="prior",
    )(prior_full, prior_rows)

    return call(
        lambda *refs: finish_kernel(n_col, *refs),
        "finish",
        struct((total_rows, own, width)),
        ids,
        w,
        q,
        to[0],
        *came,
    )


def solution(mesh):
    in_specs = (P("row", None, "col"), P(None, "row", "col"))
    out_specs = P(None, "row", "col")
    return jax.shard_map(local, mesh=mesh, in_specs=in_specs, out_specs=out_specs, check_vma=False)
```

```python
import jax
import jax.numpy as jnp
from jax import lax
from jax.experimental import pallas as pl
from jax.experimental.pallas import tpu as pltpu
from jax.sharding import PartitionSpec as P

F32 = jnp.float32
BF16 = jnp.bfloat16
HIGHEST = lax.Precision.HIGHEST
ANY_CONTRACT = (((0,), (0,)), ((), ()))


def dot_tt(a, b):
    return lax.dot_general(a, b, ANY_CONTRACT, precision=HIGHEST, preferred_element_type=F32)


def dot(a, b):
    return jnp.dot(a, b, precision=HIGHEST, preferred_element_type=F32)


def split2(x):
    hi = x.astype(BF16)
    return hi, (x - hi.astype(F32)).astype(BF16)


def split3(x):
    one = x.astype(BF16).astype(F32)
    rest = x - one
    two = rest.astype(BF16).astype(F32)
    return one, two, rest - two


def eliminate(a_ref, u_ref, n):
    sub = lax.broadcasted_iota(jnp.int32, (8, n), 0)
    for k in range(n // 8):
        lo = 8 * k
        left = a_ref[lo : lo + 8, :n]
        right = a_ref[lo : lo + 8, n:]
        rl = [jnp.broadcast_to(left[p : p + 1, :], (8, n)) for p in range(8)]
        rr = [jnp.broadcast_to(right[p : p + 1, :], (8, n)) for p in range(8)]
        d = [
            [
                jnp.broadcast_to(left[p : p + 1, lo + q : lo + q + 1], (8, n)) if q >= p else None
                for q in range(8)
            ]
            for p in range(8)
        ]
        tl = tr = None
        for p in range(8):
            inv = 1.0 / d[p][p]
            rs = lax.rsqrt(d[p][p])
            rs = rs * (1.5 - 0.5 * d[p][p] * rs * rs)
            for q in range(p + 1, 8):
                factor = d[p][q] * inv
                for s in range(q, 8):
                    d[q][s] = d[q][s] - factor * d[p][s]
                rl[q] = rl[q] - factor * rl[p]
                rr[q] = rr[q] - factor * rr[p]
            a = rl[p] * rs
            b = rr[p] * rs
            tl = a if p == 0 else jnp.where(sub == p, a, tl)
            tr = b if p == 0 else jnp.where(sub == p, b, tr)
        u_ref[lo : lo + 8, :n] = tl
        u_ref[lo : lo + 8, n:] = tr
        if k + 1 < n // 8:
            t1, t2, t3 = split3(jnp.concatenate([tl, tr], axis=1))
            lhs = jnp.concatenate([t1[:, :n], t1[:, :n], t2[:, :n], t1[:, :n], t2[:, :n], t3[:, :n]], axis=0)
            rhs = jnp.concatenate([t1, t2, t1, t3, t2, t1], axis=0)
            update = lax.dot_general(
                lhs.astype(BF16), rhs.astype(BF16), ANY_CONTRACT, preferred_element_type=F32
            )
            a_ref[lo + 8 :, :] = a_ref[lo + 8 :, :] - update[lo + 8 :, :]


def blocks(rows):
    h = rows.shape[1] // 2
    top = dot_tt(rows[:, :h], rows)
    return jnp.concatenate([top[:, :h], top[:, h:], dot_tt(rows[:, h:], rows[:, h:])], axis=0)


def factor_kernel(ids_ref, kept_ref, other_ref, w_ref, a_ref, u_ref):
    half, h = kept_ref.shape
    low = ids_ref[1] == 0
    kept = kept_ref[...]
    other = other_ref[...]
    stack = jnp.concatenate([jnp.where(low, kept, other), jnp.where(low, other, kept)], axis=0)
    eye = (
        lax.broadcasted_iota(jnp.int32, (h, h), 0) == lax.broadcasted_iota(jnp.int32, (h, h), 1)
    ).astype(F32)
    a_ref[:, :h] = stack[:h]
    a_ref[:, h:] = eye
    eliminate(a_ref, u_ref, h)
    w00 = u_ref[:, h:]
    w_ref[:h, :h] = w00
    w_ref[:h, h:] = jnp.zeros((h, h), F32)
    u01 = dot(w00, stack[h : 2 * h])
    a_ref[:, :h] = stack[2 * h :] - dot_tt(u01, u01)
    a_ref[:, h:] = eye
    x = dot_tt(u01, w00)
    eliminate(a_ref, u_ref, h)
    w11 = u_ref[:, h:]
    w_ref[h:, h:] = w11
    w_ref[h:, :h] = -dot(w11, x)


def split_kernel(ids_ref, obs_ref, hi_ref, lo_ref, next_ref, buf, sems):
    rows, cycles, width = obs_ref.shape
    own = cycles // (2 * hi_ref.shape[1])
    core = ids_ref[1]
    copies = [pltpu.make_async_copy(obs_ref.at[:, c, :], buf.at[c], sems.at[c]) for c in range(cycles)]
    for copy in copies:
        copy.start()
    for i in range(3):
        next_ref[i] = ids_ref[i]
    for c, copy in enumerate(copies):
        copy.wait()
        place, at = divmod(c, own)
        z, side = divmod(place, 2)
        hi, lo = split2(buf[c].T)
        kept = jnp.where(core == side, 1, 0)
        hi_ref[kept, z, at * width : (at + 1) * width, :] = hi
        lo_ref[kept, z, at * width : (at + 1) * width, :] = lo


def prior_kernel(own_ref, got_ref, *refs):
    *columns, out_ref = refs
    panel = own_ref[...] + got_ref[...]
    for z, ref in enumerate(columns):
        width = ref.shape[2]
        for e in range(ref.shape[1]):
            out_ref[z, e * width : (e + 1) * width, :] = dot_tt(ref[:, e, :], panel)


def pieces_kernel(obs_ref, pri_ref, out_ref, sem, psem):
    pieces, rows, width = out_ref.shape
    n = obs_ref.shape[0] // pieces
    copies = []
    for i in range(pieces):
        copies.append(
            pltpu.make_async_copy(obs_ref.at[n * i : n * (i + 1), 0, :], out_ref.at[i, :n, :], sem.at[i])
        )
        m = rows - n
        copies.append(
            pltpu.make_async_copy(pri_ref.at[m * i : m * (i + 1), 0, :], out_ref.at[i, n:, :], psem.at[i])
        )
    for copy in copies:
        copy.start()
    for copy in copies:
        copy.wait()


def assembled(z_ref, n):
    pieces, panels, rows, width = z_ref.shape
    return [
        jnp.concatenate([z_ref[:, p, a:b, :].reshape(pieces * (b - a), width) for p in range(panels)], axis=1)
        for a, b in ((0, n), (n, rows))
    ]


def gram_kernel(n, ids_ref, z_ref, keep_ref, send_ref, prior_ref):
    rows, prior = assembled(z_ref, n)
    prior_ref[...] = prior
    stack = blocks(jnp.concatenate([rows, prior], axis=0))
    half = stack.shape[0] // 2
    low = ids_ref[1] == 0
    keep_ref[...] = jnp.where(low, stack[:half], stack[half:])
    send_ref[...] = jnp.where(low, stack[half:], stack[:half])


def panel_kernel(n, ids_ref, z_ref, hi_ref, lo_ref):
    hi_ref[...], lo_ref[...] = split2(assembled(z_ref, n)[0])


def product_kernel(ids_ref, phi_ref, plo_ref, ahi_ref, alo_ref, send_ref, keep_ref):
    for side, out_ref in enumerate((send_ref, keep_ref)):
        for z in range(out_ref.shape[0]):
            out_ref[z] = (
                jnp.dot(ahi_ref[side, z], phi_ref[...], preferred_element_type=F32)
                + jnp.dot(ahi_ref[side, z], plo_ref[...], preferred_element_type=F32)
                + jnp.dot(alo_ref[side, z], phi_ref[...], preferred_element_type=F32)
            )


def combine_kernel(ids_ref, kept_ref, got_ref, prior_ref, *out_refs):
    z = ids_ref[0] // 2
    for k, out_ref in enumerate(out_refs):
        at = jnp.bitwise_xor(z, k)
        out_ref[...] = kept_ref[at] + got_ref[at] + prior_ref[at]


def finish_kernel(n_col, ids_ref, w_ref, *refs):
    out_ref = refs[-1]
    rows, own, width = out_ref.shape
    part = [ref[...] for ref in refs[:-1]]
    while len(part) > 1:
        part = [a + b for a, b in zip(part[::2], part[1::2])] + part[len(part) // 2 * 2 :]
    coeffs = lax.dot_general(
        w_ref[...], part[0], (((1,), (1,)), ((), ())), precision=HIGHEST, preferred_element_type=F32
    )
    panel = lax.broadcasted_iota(jnp.int32, (rows, width), 0) // width
    for c in range(own):
        block = (ids_ref[0] * own + c) * n_col + ids_ref[2]
        out_ref[:, c, :] = jnp.where(block >= panel, coeffs[:, c * width : (c + 1) * width], 0.0)


def smem():
    return pl.BlockSpec(memory_space=pltpu.SMEM)


def vmem():
    return pl.BlockSpec(memory_space=pltpu.VMEM)


def anywhere():
    return pl.BlockSpec(memory_space=pltpu.HBM)


def call(kernel, name, us, out_shape, *args, ids=None, specs=None, outs=None, scratch=(), limit=32 << 20):
    specs = specs or [vmem()] * len(args)
    first = () if ids is None else (ids,)
    return pl.pallas_call(
        kernel,
        out_shape=out_shape,
        in_specs=[smem()] * len(first) + specs,
        out_specs=outs or jax.tree.map(lambda _: vmem(), out_shape),
        scratch_shapes=list(scratch),
        compiler_params=pltpu.CompilerParams(vmem_limit_bytes=limit),
        cost_estimate=pl.CostEstimate(flops=0, bytes_accessed=int(us * 3.6e6), transcendentals=0),
        name=name,
    )(*first, *args)


def gated(x, after):
    return lax.optimization_barrier((x, after))[0]


def inhbm(x):
    return pltpu.with_memory_space_constraint(x, pltpu.HBM)


def held(shape, dtype):
    return pltpu.VMEM(shape, dtype)


def struct(shape, dtype=F32):
    return jax.ShapeDtypeStruct(shape, dtype)


def local(observations, prior_rows):
    obs, cycles, width = observations.shape
    total_rows, own, _ = prior_rows.shape
    panels = total_rows // width
    n_row = lax.axis_size("row")
    n_col = lax.axis_size("col")
    plane = n_col // 2
    places = n_row // 2
    wide = panels * width
    pairs = cycles // own
    row_pos = lax.axis_index("row")
    col_pos = lax.axis_index("col")
    ids = jnp.stack([row_pos, row_pos % 2, col_pos]).astype(jnp.int32)
    planes = [[h * plane + i for i in range(plane)] for h in range(2)]

    def exchange(x):
        return lax.all_to_all(x, "col", 0, 0, tiled=True, axis_index_groups=planes)

    def share(x):
        return exchange(jnp.broadcast_to(x[None], (plane,) + x.shape))

    def swap(x, k):
        return lax.ppermute(x, "row", [(r, r ^ k) for r in range(n_row)])

    def across(x):
        far = lax.ppermute(x, "col", [(i, i + plane) for i in range(plane)])
        return jnp.where(col_pos >= plane, far, x)

    each = obs // plane
    pieces = call(
        pieces_kernel,
        "pieces",
        2,
        struct((plane, each + total_rows // plane, width)),
        inhbm(observations),
        inhbm(prior_rows),
        specs=[anywhere()] * 2,
        scratch=[pltpu.SemaphoreType.DMA((plane,))] * 2,
    )
    got = exchange(pieces)[:panels]
    holder = 2
    moved = [
        lax.ppermute(
            got[:, each:, :],
            ("row", "col"),
            [(c, holder * n_col + c + h * plane) for c in range(plane)],
        )
        for h in range(2)
    ]
    rows = across(got[:, :each, :])
    prior = jnp.where(ids[0] == holder, moved[0] + moved[1], 0.0)
    ids, full = lax.optimization_barrier((ids, jnp.concatenate([rows, prior], axis=1)))
    gathered = share(full)
    ahi, alo, ids = call(
        split_kernel,
        "split",
        6,
        [held((2, places, own * width, obs), BF16)] * 2 + [struct((3,), jnp.int32)],
        inhbm(observations),
        ids=ids,
        specs=[anywhere()],
        outs=[vmem(), vmem(), smem()],
        scratch=[pltpu.VMEM((cycles, obs, width), F32), pltpu.SemaphoreType.DMA((cycles,))],
    )
    columns = [
        prior_rows
        if 2 * z == holder
        else lax.ppermute(prior_rows, "row", [(2 * z + core, holder + core) for core in range(2)])
        for z in range(places)
    ]

    gathered, ids, *columns = lax.optimization_barrier((gathered, ids, *columns))
    gram_keep, gram_send, prior_panel = call(
        lambda *refs: gram_kernel(each, *refs),
        "gram",
        1.5,
        [struct((3 * width // 2, width))] * 2 + [struct((total_rows, wide))],
        gathered,
        ids=ids,
    )
    gram_got = swap(gram_send, 1)
    panel = call(
        lambda *refs: panel_kernel(each, *refs),
        "panel",
        0.4,
        [struct((obs, wide), BF16)] * 2,
        gathered,
        ids=gated(ids, gram_send),
    )

    prior_sums = call(
        prior_kernel,
        "prior",
        2,
        struct((places, own * width, wide)),
        prior_panel,
        lax.ppermute(prior_panel, "row", [(holder, holder + 1)]),
        *columns,
    )

    gram = gram_keep + gram_got
    gram_far = [swap(gram, 2 * k) for k in range(1, places)]
    sums_send, sums_keep = call(
        product_kernel,
        "product",
        7,
        [struct((places, own * width, wide))] * 2,
        *panel,
        pltpu.with_memory_space_constraint(ahi, pltpu.VMEM),
        pltpu.with_memory_space_constraint(alo, pltpu.VMEM),
        ids=gated(ids, gram),
    )
    sums_got = swap(sums_send, 1)
    gram = (gram + gram_far[0]) + (gram_far[1] + gram_far[2])
    gram_other = swap(gram, 1)
    to = call(
        combine_kernel,
        "combine",
        0.6,
        [struct((own * width, wide))] * places,
        sums_keep,
        sums_got,
        prior_sums,
        ids=ids,
    )
    came = [swap(to[k], 2 * k) for k in range(1, places)]
    w = call(
        factor_kernel,
        "factor",
        13,
        struct((wide, wide)),
        gram,
        gram_other,
        ids=ids,
        scratch=[pltpu.VMEM((wide // 2, wide), F32)] * 2,
    )
    return call(
        lambda *refs: finish_kernel(n_col, *refs),
        "finish",
        2,
        struct((total_rows, own, width)),
        w,
        to[0],
        *came,
        ids=ids,
    )


def solution(mesh):
    in_specs = (P("row", None, "col"), P(None, "row", "col"))
    out_specs = P(None, "row", "col")
    return jax.shard_map(local, mesh=mesh, in_specs=in_specs, out_specs=out_specs, check_vma=False)
```

```python
import jax
import jax.numpy as jnp
from jax import lax
from jax.experimental import pallas as pl
from jax.experimental.pallas import tpu as pltpu
from jax.sharding import PartitionSpec as P

F32 = jnp.float32
BF16 = jnp.bfloat16
HIGHEST = lax.Precision.HIGHEST
ANY_CONTRACT = (((0,), (0,)), ((), ()))


def dot_tt(a, b):
    return lax.dot_general(a, b, ANY_CONTRACT, precision=HIGHEST, preferred_element_type=F32)


def dot(a, b):
    return jnp.dot(a, b, precision=HIGHEST, preferred_element_type=F32)


def split2(x):
    hi = x.astype(BF16)
    return hi, (x - hi.astype(F32)).astype(BF16)


def split3(x):
    one = x.astype(BF16).astype(F32)
    rest = x - one
    two = rest.astype(BF16).astype(F32)
    return one, two, rest - two


def eliminate(a_ref, u_ref, n):
    sub = lax.broadcasted_iota(jnp.int32, (8, n), 0)
    for k in range(n // 8):
        lo = 8 * k
        left = a_ref[lo : lo + 8, :n]
        right = a_ref[lo : lo + 8, n:]
        rl = [jnp.broadcast_to(left[p : p + 1, :], (8, n)) for p in range(8)]
        rr = [jnp.broadcast_to(right[p : p + 1, :], (8, n)) for p in range(8)]
        d = [
            [
                jnp.broadcast_to(left[p : p + 1, lo + q : lo + q + 1], (8, n)) if q >= p else None
                for q in range(8)
            ]
            for p in range(8)
        ]
        tl = tr = None
        for p in range(8):
            inv = 1.0 / d[p][p]
            rs = lax.rsqrt(d[p][p])
            rs = rs * (1.5 - 0.5 * d[p][p] * rs * rs)
            for q in range(p + 1, 8):
                factor = d[p][q] * inv
                for s in range(q, 8):
                    d[q][s] = d[q][s] - factor * d[p][s]
                rl[q] = rl[q] - factor * rl[p]
                rr[q] = rr[q] - factor * rr[p]
            a = rl[p] * rs
            b = rr[p] * rs
            tl = a if p == 0 else jnp.where(sub == p, a, tl)
            tr = b if p == 0 else jnp.where(sub == p, b, tr)
        u_ref[lo : lo + 8, :n] = tl
        u_ref[lo : lo + 8, n:] = tr
        if k + 1 < n // 8:
            t1, t2, t3 = split3(jnp.concatenate([tl, tr], axis=1))
            lhs = jnp.concatenate([t1[:, :n], t1[:, :n], t2[:, :n], t1[:, :n], t2[:, :n], t3[:, :n]], axis=0)
            rhs = jnp.concatenate([t1, t2, t1, t3, t2, t1], axis=0)
            update = lax.dot_general(
                lhs.astype(BF16), rhs.astype(BF16), ANY_CONTRACT, preferred_element_type=F32
            )
            a_ref[lo + 8 :, :] = a_ref[lo + 8 :, :] - update[lo + 8 :, :]


def blocks(rows):
    h = rows.shape[1] // 2
    top = dot_tt(rows[:, :h], rows)
    return jnp.concatenate([top[:, :h], top[:, h:], dot_tt(rows[:, h:], rows[:, h:])], axis=0)


def factor_kernel(ids_ref, kept_ref, other_ref, w_ref, a_ref, u_ref):
    half, h = kept_ref.shape
    low = ids_ref[1] == 0
    kept = kept_ref[...]
    other = other_ref[...]
    stack = jnp.concatenate([jnp.where(low, kept, other), jnp.where(low, other, kept)], axis=0)
    eye = (
        lax.broadcasted_iota(jnp.int32, (h, h), 0) == lax.broadcasted_iota(jnp.int32, (h, h), 1)
    ).astype(F32)
    a_ref[:, :h] = stack[:h]
    a_ref[:, h:] = eye
    eliminate(a_ref, u_ref, h)
    w00 = u_ref[:, h:]
    w_ref[:h, :h] = w00
    w_ref[:h, h:] = jnp.zeros((h, h), F32)
    u01 = dot(w00, stack[h : 2 * h])
    a_ref[:, :h] = stack[2 * h :] - dot_tt(u01, u01)
    a_ref[:, h:] = eye
    x = dot_tt(u01, w00)
    eliminate(a_ref, u_ref, h)
    w11 = u_ref[:, h:]
    w_ref[h:, h:] = w11
    w_ref[h:, :h] = -dot(w11, x)


def split_kernel(ids_ref, obs_ref, send_hi_ref, send_lo_ref, keep_hi_ref, keep_lo_ref, next_ref, buf, sems):
    rows, cycles, width = obs_ref.shape
    own = cycles // (2 * send_hi_ref.shape[0])
    core = ids_ref[1]
    copies = [pltpu.make_async_copy(obs_ref.at[:, c, :], buf.at[c], sems.at[c]) for c in range(cycles)]
    for copy in copies:
        copy.start()
    for i in range(3):
        next_ref[i] = ids_ref[i]

    def place(c, hi_ref, lo_ref):
        place, at = divmod(c, own)
        hi, lo = split2(buf[c].T)
        hi_ref[place // 2, at * width : (at + 1) * width, :] = hi
        lo_ref[place // 2, at * width : (at + 1) * width, :] = lo

    for c in range(0, cycles, 2 * own):
        for copy in copies[c : c + 2 * own]:
            copy.wait()
        for side in range(2):

            @pl.when(core == side)
            def _():
                for e in range(own):
                    place(c + side * own + e, keep_hi_ref, keep_lo_ref)
                    place(c + (1 - side) * own + e, send_hi_ref, send_lo_ref)


def prior_kernel(own_ref, got_ref, *refs):
    *columns, out_ref = refs
    panel = own_ref[...] + got_ref[...]
    for z, ref in enumerate(columns):
        width = ref.shape[2]
        for e in range(ref.shape[1]):
            out_ref[z, e * width : (e + 1) * width, :] = dot_tt(ref[:, e, :], panel)


def pieces_kernel(obs_ref, pri_ref, out_ref, sem, psem):
    pieces, rows, width = out_ref.shape
    n = obs_ref.shape[0] // pieces
    copies = []
    for i in range(pieces):
        copies.append(
            pltpu.make_async_copy(obs_ref.at[n * i : n * (i + 1), 0, :], out_ref.at[i, :n, :], sem.at[i])
        )
        m = rows - n
        copies.append(
            pltpu.make_async_copy(pri_ref.at[m * i : m * (i + 1), 0, :], out_ref.at[i, n:, :], psem.at[i])
        )
    for copy in copies:
        copy.start()
    for copy in copies:
        copy.wait()


def assembled(z_ref, n):
    pieces, panels, rows, width = z_ref.shape
    return [
        jnp.concatenate([z_ref[:, p, a:b, :].reshape(pieces * (b - a), width) for p in range(panels)], axis=1)
        for a, b in ((0, n), (n, rows))
    ]


def gram_kernel(n, ids_ref, z_ref, keep_ref, send_ref, prior_ref):
    rows, prior = assembled(z_ref, n)
    prior_ref[...] = prior
    stack = blocks(jnp.concatenate([rows, prior], axis=0))
    half = stack.shape[0] // 2
    low = ids_ref[1] == 0
    keep_ref[...] = jnp.where(low, stack[:half], stack[half:])
    send_ref[...] = jnp.where(low, stack[half:], stack[:half])


def panel_kernel(n, ids_ref, z_ref, hi_ref, lo_ref):
    hi_ref[...], lo_ref[...] = split2(assembled(z_ref, n)[0])


def product_kernel(ids_ref, phi_ref, plo_ref, ahi_ref, alo_ref, out_ref):
    for z in range(out_ref.shape[0]):
        out_ref[z] = (
            jnp.dot(ahi_ref[z], phi_ref[...], preferred_element_type=F32)
            + jnp.dot(ahi_ref[z], plo_ref[...], preferred_element_type=F32)
            + jnp.dot(alo_ref[z], phi_ref[...], preferred_element_type=F32)
        )


def combine_kernel(ids_ref, kept_ref, got_ref, prior_ref, *out_refs):
    z = ids_ref[0] // 2
    for k, out_ref in enumerate(out_refs):
        at = jnp.bitwise_xor(z, k)
        out_ref[...] = kept_ref[at] + got_ref[at] + prior_ref[at]


def finish_kernel(n_col, ids_ref, w_ref, *refs):
    out_ref = refs[-1]
    rows, own, width = out_ref.shape
    part = [ref[...] for ref in refs[:-1]]
    while len(part) > 1:
        part = [a + b for a, b in zip(part[::2], part[1::2])] + part[len(part) // 2 * 2 :]
    coeffs = lax.dot_general(
        w_ref[...], part[0], (((1,), (1,)), ((), ())), precision=HIGHEST, preferred_element_type=F32
    )
    panel = lax.broadcasted_iota(jnp.int32, (rows, width), 0) // width
    for c in range(own):
        block = (ids_ref[0] * own + c) * n_col + ids_ref[2]
        out_ref[:, c, :] = jnp.where(block >= panel, coeffs[:, c * width : (c + 1) * width], 0.0)


def smem():
    return pl.BlockSpec(memory_space=pltpu.SMEM)


def vmem():
    return pl.BlockSpec(memory_space=pltpu.VMEM)


def anywhere():
    return pl.BlockSpec(memory_space=pltpu.HBM)


def call(kernel, name, us, out_shape, *args, ids=None, specs=None, outs=None, scratch=(), limit=32 << 20):
    specs = specs or [vmem()] * len(args)
    first = () if ids is None else (ids,)
    return pl.pallas_call(
        kernel,
        out_shape=out_shape,
        in_specs=[smem()] * len(first) + specs,
        out_specs=outs or jax.tree.map(lambda _: vmem(), out_shape),
        scratch_shapes=list(scratch),
        compiler_params=pltpu.CompilerParams(vmem_limit_bytes=limit),
        cost_estimate=pl.CostEstimate(flops=0, bytes_accessed=int(us * 3.6e6), transcendentals=0),
        name=name,
    )(*first, *args)


def gated(x, after):
    return lax.optimization_barrier((x, after))[0]


def inhbm(x):
    return pltpu.with_memory_space_constraint(x, pltpu.HBM)


def held(shape, dtype):
    return pltpu.VMEM(shape, dtype)


def struct(shape, dtype=F32):
    return jax.ShapeDtypeStruct(shape, dtype)


def local(observations, prior_rows):
    obs, cycles, width = observations.shape
    total_rows, own, _ = prior_rows.shape
    panels = total_rows // width
    n_row = lax.axis_size("row")
    n_col = lax.axis_size("col")
    plane = n_col // 2
    places = n_row // 2
    wide = panels * width
    pairs = cycles // own
    row_pos = lax.axis_index("row")
    col_pos = lax.axis_index("col")
    ids = jnp.stack([row_pos, row_pos % 2, col_pos]).astype(jnp.int32)
    planes = [[h * plane + i for i in range(plane)] for h in range(2)]

    def exchange(x):
        return lax.all_to_all(x, "col", 0, 0, tiled=True, axis_index_groups=planes)

    def share(x):
        return exchange(jnp.broadcast_to(x[None], (plane,) + x.shape))

    def swap(x, k):
        return lax.ppermute(x, "row", [(r, r ^ k) for r in range(n_row)])

    def across(x):
        far = lax.ppermute(x, "col", [(i, i + plane) for i in range(plane)])
        return jnp.where(col_pos >= plane, far, x)

    each = obs // plane
    pieces = call(
        pieces_kernel,
        "pieces",
        2,
        struct((plane, each + total_rows // plane, width)),
        inhbm(observations),
        inhbm(prior_rows),
        specs=[anywhere()] * 2,
        scratch=[pltpu.SemaphoreType.DMA((plane,))] * 2,
    )
    got = exchange(pieces)[:panels]
    holder = 2
    moved = [
        lax.ppermute(
            got[:, each:, :],
            ("row", "col"),
            [(c, holder * n_col + c + h * plane) for c in range(plane)],
        )
        for h in range(2)
    ]
    rows = across(got[:, :each, :])
    prior = jnp.where(ids[0] == holder, moved[0] + moved[1], 0.0)
    ids, full = lax.optimization_barrier((ids, jnp.concatenate([rows, prior], axis=1)))
    gathered = share(full)
    *turned, ids = call(
        split_kernel,
        "split",
        6,
        [held((places, own * width, obs), BF16)] * 4 + [struct((3,), jnp.int32)],
        inhbm(observations),
        ids=ids,
        specs=[anywhere()],
        outs=[vmem()] * 4 + [smem()],
        scratch=[pltpu.VMEM((cycles, obs, width), F32), pltpu.SemaphoreType.DMA((cycles,))],
    )
    columns = [
        prior_rows
        if 2 * z == holder
        else lax.ppermute(prior_rows, "row", [(2 * z + core, holder + core) for core in range(2)])
        for z in range(places)
    ]

    gathered, ids, *columns = lax.optimization_barrier((gathered, ids, *columns))
    gram_keep, gram_send, prior_panel = call(
        lambda *refs: gram_kernel(each, *refs),
        "gram",
        1.5,
        [struct((3 * width // 2, width))] * 2 + [struct((total_rows, wide))],
        gathered,
        ids=ids,
    )
    gram_got = swap(gram_send, 1)
    panel = call(
        lambda *refs: panel_kernel(each, *refs),
        "panel",
        0.4,
        [struct((obs, wide), BF16)] * 2,
        gathered,
        ids=gated(ids, gram_send),
    )

    prior_sums = call(
        prior_kernel,
        "prior",
        0.1,
        struct((places, own * width, wide)),
        prior_panel,
        lax.ppermute(prior_panel, "row", [(holder, holder + 1)]),
        *columns,
    )

    gram = gram_keep + gram_got
    gram_far = [swap(gram, 2 * k) for k in range(1, places)]
    def product(parts, after, name):
        return call(
            product_kernel,
            name,
            0.1,
            struct((places, own * width, wide)),
            *panel,
            *[pltpu.with_memory_space_constraint(x, pltpu.VMEM) for x in parts],
            ids=gated(ids, after),
        )

    sums_send = product(turned[:2], gram, "product_send")
    sums_got = swap(sums_send, 1)
    sums_keep = product(turned[2:], sums_send, "product_keep")
    gram = (gram + gram_far[0]) + (gram_far[1] + gram_far[2])
    gram_other = swap(gram, 1)
    to = call(
        combine_kernel,
        "combine",
        0.1,
        [struct((own * width, wide))] * places,
        sums_keep,
        sums_got,
        prior_sums,
        ids=ids,
    )
    came = [swap(to[k], 2 * k) for k in range(1, places)]
    w = call(
        factor_kernel,
        "factor",
        13,
        struct((wide, wide)),
        gram,
        gram_other,
        ids=ids,
        scratch=[pltpu.VMEM((wide // 2, wide), F32)] * 2,
    )
    return call(
        lambda *refs: finish_kernel(n_col, *refs),
        "finish",
        2,
        struct((total_rows, own, width)),
        w,
        to[0],
        *came,
        ids=ids,
    )


def solution(mesh):
    in_specs = (P("row", None, "col"), P(None, "row", "col"))
    out_specs = P(None, "row", "col")
    return jax.shard_map(local, mesh=mesh, in_specs=in_specs, out_specs=out_specs, check_vma=False)
```

```python
import jax
import jax.numpy as jnp
from jax import lax
from jax.experimental import pallas as pl
from jax.experimental.pallas import tpu as pltpu
from jax.sharding import PartitionSpec as P

F32 = jnp.float32
BF16 = jnp.bfloat16
HIGHEST = lax.Precision.HIGHEST
ANY_CONTRACT = (((0,), (0,)), ((), ()))


def dot_tt(a, b):
    return lax.dot_general(a, b, ANY_CONTRACT, precision=HIGHEST, preferred_element_type=F32)


def dot(a, b):
    return jnp.dot(a, b, precision=HIGHEST, preferred_element_type=F32)


def split2(x):
    hi = x.astype(BF16)
    return hi, (x - hi.astype(F32)).astype(BF16)


def split3(x):
    one = x.astype(BF16).astype(F32)
    rest = x - one
    two = rest.astype(BF16).astype(F32)
    return one, two, rest - two


def eliminate(a_ref, u_ref, n):
    sub = lax.broadcasted_iota(jnp.int32, (8, n), 0)
    for k in range(n // 8):
        lo = 8 * k
        left = a_ref[lo : lo + 8, :n]
        right = a_ref[lo : lo + 8, n:]
        rl = [jnp.broadcast_to(left[p : p + 1, :], (8, n)) for p in range(8)]
        rr = [jnp.broadcast_to(right[p : p + 1, :], (8, n)) for p in range(8)]
        d = [
            [
                jnp.broadcast_to(left[p : p + 1, lo + q : lo + q + 1], (8, n)) if q >= p else None
                for q in range(8)
            ]
            for p in range(8)
        ]
        tl = tr = None
        for p in range(8):
            inv = 1.0 / d[p][p]
            rs = lax.rsqrt(d[p][p])
            rs = rs * (1.5 - 0.5 * d[p][p] * rs * rs)
            for q in range(p + 1, 8):
                factor = d[p][q] * inv
                for s in range(q, 8):
                    d[q][s] = d[q][s] - factor * d[p][s]
                rl[q] = rl[q] - factor * rl[p]
                rr[q] = rr[q] - factor * rr[p]
            a = rl[p] * rs
            b = rr[p] * rs
            tl = a if p == 0 else jnp.where(sub == p, a, tl)
            tr = b if p == 0 else jnp.where(sub == p, b, tr)
        u_ref[lo : lo + 8, :n] = tl
        u_ref[lo : lo + 8, n:] = tr
        if k + 1 < n // 8:
            t1, t2, t3 = split3(jnp.concatenate([tl, tr], axis=1))
            lhs = jnp.concatenate([t1[:, :n], t1[:, :n], t2[:, :n], t1[:, :n], t2[:, :n], t3[:, :n]], axis=0)
            rhs = jnp.concatenate([t1, t2, t1, t3, t2, t1], axis=0)
            update = lax.dot_general(
                lhs.astype(BF16), rhs.astype(BF16), ANY_CONTRACT, preferred_element_type=F32
            )
            a_ref[lo + 8 :, :] = a_ref[lo + 8 :, :] - update[lo + 8 :, :]


def blocks(rows):
    h = rows.shape[1] // 2
    top = dot_tt(rows[:, :h], rows)
    return jnp.concatenate([top[:, :h], top[:, h:], dot_tt(rows[:, h:], rows[:, h:])], axis=0)


def factor_kernel(ids_ref, kept_ref, other_ref, w_ref, a_ref, u_ref):
    half, h = kept_ref.shape
    low = ids_ref[1] == 0
    kept = kept_ref[...]
    other = other_ref[...]
    stack = jnp.concatenate([jnp.where(low, kept, other), jnp.where(low, other, kept)], axis=0)
    eye = (
        lax.broadcasted_iota(jnp.int32, (h, h), 0) == lax.broadcasted_iota(jnp.int32, (h, h), 1)
    ).astype(F32)
    a_ref[:, :h] = stack[:h]
    a_ref[:, h:] = eye
    eliminate(a_ref, u_ref, h)
    w00 = u_ref[:, h:]
    w_ref[:h, :h] = w00
    w_ref[:h, h:] = jnp.zeros((h, h), F32)
    u01 = dot(w00, stack[h : 2 * h])
    a_ref[:, :h] = stack[2 * h :] - dot_tt(u01, u01)
    a_ref[:, h:] = eye
    x = dot_tt(u01, w00)
    eliminate(a_ref, u_ref, h)
    w11 = u_ref[:, h:]
    w_ref[h:, h:] = w11
    w_ref[h:, :h] = -dot(w11, x)


def split_kernel(ids_ref, obs_ref, send_hi_ref, send_lo_ref, keep_hi_ref, keep_lo_ref, next_ref, buf, sems):
    rows, cycles, width = obs_ref.shape
    own = cycles // (2 * send_hi_ref.shape[0])
    core = ids_ref[1]
    copies = [pltpu.make_async_copy(obs_ref.at[:, c, :], buf.at[c], sems.at[c]) for c in range(cycles)]
    for copy in copies:
        copy.start()
    for i in range(3):
        next_ref[i] = ids_ref[i]

    def place(c, hi_ref, lo_ref):
        place, at = divmod(c, own)
        hi, lo = split2(buf[c].T)
        hi_ref[place // 2, at * width : (at + 1) * width, :] = hi
        lo_ref[place // 2, at * width : (at + 1) * width, :] = lo

    for c in range(0, cycles, 2 * own):
        for copy in copies[c : c + 2 * own]:
            copy.wait()
        for side in range(2):

            @pl.when(core == side)
            def _():
                for e in range(own):
                    place(c + side * own + e, keep_hi_ref, keep_lo_ref)
                    place(c + (1 - side) * own + e, send_hi_ref, send_lo_ref)


def prior_kernel(own_ref, got_ref, *refs):
    *columns, out_ref = refs
    panel = own_ref[...] + got_ref[...]
    for z, ref in enumerate(columns):
        width = ref.shape[2]
        for e in range(ref.shape[1]):
            out_ref[z, e * width : (e + 1) * width, :] = dot_tt(ref[:, e, :], panel)


def pieces_kernel(obs_ref, pri_ref, out_ref, sem, psem):
    pieces, rows, width = out_ref.shape
    n = obs_ref.shape[0] // pieces
    copies = []
    for i in range(pieces):
        copies.append(
            pltpu.make_async_copy(obs_ref.at[n * i : n * (i + 1), 0, :], out_ref.at[i, :n, :], sem.at[i])
        )
        m = rows - n
        copies.append(
            pltpu.make_async_copy(pri_ref.at[m * i : m * (i + 1), 0, :], out_ref.at[i, n:, :], psem.at[i])
        )
    for copy in copies:
        copy.start()
    for copy in copies:
        copy.wait()


def assembled(z_ref, n):
    pieces, panels, rows, width = z_ref.shape
    return [
        jnp.concatenate([z_ref[:, p, a:b, :].reshape(pieces * (b - a), width) for p in range(panels)], axis=1)
        for a, b in ((0, n), (n, rows))
    ]


def gram_kernel(n, ids_ref, z_ref, keep_ref, send_ref, prior_ref):
    rows, prior = assembled(z_ref, n)
    prior_ref[...] = prior
    stack = blocks(jnp.concatenate([rows, prior], axis=0))
    half = stack.shape[0] // 2
    low = ids_ref[1] == 0
    keep_ref[...] = jnp.where(low, stack[:half], stack[half:])
    send_ref[...] = jnp.where(low, stack[half:], stack[:half])


def panel_kernel(n, ids_ref, z_ref, hi_ref, lo_ref):
    hi_ref[...], lo_ref[...] = split2(assembled(z_ref, n)[0])


def product_kernel(ids_ref, phi_ref, plo_ref, ahi_ref, alo_ref, out_ref):
    for z in range(out_ref.shape[0]):
        out_ref[z] = (
            jnp.dot(ahi_ref[z], phi_ref[...], preferred_element_type=F32)
            + jnp.dot(ahi_ref[z], plo_ref[...], preferred_element_type=F32)
            + jnp.dot(alo_ref[z], phi_ref[...], preferred_element_type=F32)
        )


def combine_kernel(ids_ref, kept_ref, got_ref, prior_ref, *out_refs):
    z = ids_ref[0] // 2
    for k, out_ref in enumerate(out_refs):
        at = jnp.bitwise_xor(z, k)
        out_ref[...] = kept_ref[at] + got_ref[at] + prior_ref[at]


def finish_kernel(n_col, ids_ref, w_ref, *refs):
    out_ref = refs[-1]
    rows, own, width = out_ref.shape
    part = [ref[...] for ref in refs[:-1]]
    while len(part) > 1:
        part = [a + b for a, b in zip(part[::2], part[1::2])] + part[len(part) // 2 * 2 :]
    coeffs = lax.dot_general(
        w_ref[...], part[0], (((1,), (1,)), ((), ())), precision=HIGHEST, preferred_element_type=F32
    )
    panel = lax.broadcasted_iota(jnp.int32, (rows, width), 0) // width
    for c in range(own):
        block = (ids_ref[0] * own + c) * n_col + ids_ref[2]
        out_ref[:, c, :] = jnp.where(block >= panel, coeffs[:, c * width : (c + 1) * width], 0.0)


def smem():
    return pl.BlockSpec(memory_space=pltpu.SMEM)


def vmem():
    return pl.BlockSpec(memory_space=pltpu.VMEM)


def anywhere():
    return pl.BlockSpec(memory_space=pltpu.HBM)


def call(kernel, name, us, out_shape, *args, ids=None, specs=None, outs=None, scratch=(), limit=32 << 20):
    specs = specs or [vmem()] * len(args)
    first = () if ids is None else (ids,)
    return pl.pallas_call(
        kernel,
        out_shape=out_shape,
        in_specs=[smem()] * len(first) + specs,
        out_specs=outs or jax.tree.map(lambda _: vmem(), out_shape),
        scratch_shapes=list(scratch),
        compiler_params=pltpu.CompilerParams(vmem_limit_bytes=limit),
        cost_estimate=pl.CostEstimate(flops=0, bytes_accessed=int(us * 3.6e6), transcendentals=0),
        name=name,
    )(*first, *args)


def gated(x, after):
    return lax.optimization_barrier((x, after))[0]


def inhbm(x):
    return pltpu.with_memory_space_constraint(x, pltpu.HBM)


def held(shape, dtype):
    return pltpu.VMEM(shape, dtype)


def struct(shape, dtype=F32):
    return jax.ShapeDtypeStruct(shape, dtype)


def local(observations, prior_rows):
    obs, cycles, width = observations.shape
    total_rows, own, _ = prior_rows.shape
    panels = total_rows // width
    n_row = lax.axis_size("row")
    n_col = lax.axis_size("col")
    plane = n_col // 2
    places = n_row // 2
    wide = panels * width
    pairs = cycles // own
    row_pos = lax.axis_index("row")
    col_pos = lax.axis_index("col")
    ids = jnp.stack([row_pos, row_pos % 2, col_pos]).astype(jnp.int32)
    planes = [[h * plane + i for i in range(plane)] for h in range(2)]

    def exchange(x):
        return lax.all_to_all(x, "col", 0, 0, tiled=True, axis_index_groups=planes)

    def share(x):
        return exchange(jnp.broadcast_to(x[None], (plane,) + x.shape))

    def swap(x, k):
        return lax.ppermute(x, "row", [(r, r ^ k) for r in range(n_row)])

    def across(x):
        far = lax.ppermute(x, "col", [(i, i + plane) for i in range(plane)])
        return jnp.where(col_pos >= plane, far, x)

    each = obs // plane
    pieces = call(
        pieces_kernel,
        "pieces",
        2,
        struct((plane, each + total_rows // plane, width)),
        inhbm(observations),
        inhbm(prior_rows),
        specs=[anywhere()] * 2,
        scratch=[pltpu.SemaphoreType.DMA((plane,))] * 2,
    )
    got = exchange(pieces)[:panels]
    holder = 0
    prior_at = lax.broadcasted_iota(jnp.int32, got.shape, 1) >= each
    full = jnp.where(prior_at & (row_pos != holder), 0.0, across(got))
    ids, full = lax.optimization_barrier((ids, full))
    gathered = share(full)
    *turned, ids = call(
        split_kernel,
        "split",
        6,
        [held((places, own * width, obs), BF16)] * 4 + [struct((3,), jnp.int32)],
        inhbm(observations),
        ids=ids,
        specs=[anywhere()],
        outs=[vmem()] * 4 + [smem()],
        scratch=[pltpu.VMEM((cycles, obs, width), F32), pltpu.SemaphoreType.DMA((cycles,))],
    )
    columns = [
        prior_rows
        if 2 * z == holder
        else lax.ppermute(prior_rows, "row", [(2 * z + core, holder + core) for core in range(2)])
        for z in range(places)
    ]

    gathered, ids, columns[1] = lax.optimization_barrier((gathered, ids, columns[1]))
    gram_keep, gram_send, prior_panel = call(
        lambda *refs: gram_kernel(each, *refs),
        "gram",
        1.5,
        [struct((3 * width // 2, width))] * 2 + [struct((total_rows, wide))],
        gathered,
        ids=ids,
    )
    gram_got = swap(gram_send, 1)
    panel = call(
        lambda *refs: panel_kernel(each, *refs),
        "panel",
        0.4,
        [struct((obs, wide), BF16)] * 2,
        gathered,
        ids=gated(ids, gram_send),
    )

    prior_sums = call(
        prior_kernel,
        "prior",
        0.1,
        struct((places, own * width, wide)),
        prior_panel,
        lax.ppermute(prior_panel, "row", [(holder, holder + 1)]),
        *columns,
    )

    gram = gram_keep + gram_got
    gram_far = [swap(gram, 2 * k) for k in range(1, places)]
    def product(parts, after, name):
        return call(
            product_kernel,
            name,
            0.1,
            struct((places, own * width, wide)),
            *panel,
            *[pltpu.with_memory_space_constraint(x, pltpu.VMEM) for x in parts],
            ids=gated(ids, after),
        )

    gram, columns[2], columns[3] = lax.optimization_barrier((gram, columns[2], columns[3]))
    sums_send = product(turned[:2], gram, "product_send")
    sums_got = swap(sums_send, 1)
    sums_keep = product(turned[2:], sums_send, "product_keep")
    gram = (gram + gram_far[0]) + (gram_far[1] + gram_far[2])
    gram_other = swap(gram, 1)
    to = call(
        combine_kernel,
        "combine",
        0.1,
        [struct((own * width, wide))] * places,
        sums_keep,
        sums_got,
        prior_sums,
        ids=ids,
    )
    came = [swap(to[k], 2 * k) for k in range(1, places)]
    w = call(
        factor_kernel,
        "factor",
        13,
        struct((wide, wide)),
        gram,
        gram_other,
        ids=ids,
        scratch=[pltpu.VMEM((wide // 2, wide), F32)] * 2,
    )
    return call(
        lambda *refs: finish_kernel(n_col, *refs),
        "finish",
        2,
        struct((total_rows, own, width)),
        w,
        to[0],
        *came,
        ids=ids,
    )


def solution(mesh):
    in_specs = (P("row", None, "col"), P(None, "row", "col"))
    out_specs = P(None, "row", "col")
    return jax.shard_map(local, mesh=mesh, in_specs=in_specs, out_specs=out_specs, check_vma=False)
```
